256 devices in a mesh: rows: 64 (over z, x, core), sub: 4 (over y).
Axes of the slice: x: 4, y: 4, z: 8, core: 2. Of those that a mesh axis runs over, the one named last changes fastest.
Arguments:
- points: bfloat16 [262144, 256], P(('rows', 'sub')), may hold values from -1.5 to 1.5
- init_dist: float32 [262144], P(('rows', 'sub')), may hold values from 0.5 to 6
- picks: int32 [3, 4096], P(None, ('rows', 'sub')), may hold values from 0 to 1023, as said below
- pick_counts: int32 [3, 256], P(None, ('rows', 'sub')), may hold values from 1 to 16, as said below
Outputs:
- min_dist: float32 [262144], P(('rows', 'sub'))
- normalized: float32 [262144], P(('rows', 'sub'))
- round_costs: float32 [3], replicated
The draws below stay inside these ranges and needn't reach their ends.
Inputs may be any that keep to these rules, and one draw needn't show every extreme that they name: `picks`: local row numbers of the picking device; slots past that device's count hold arbitrary row numbers. `pick_counts`: in every round some device has exactly 16 live slots.
All inputs are finite; a program needn't handle non-finite values.
Results may differ from the reference program's by a relative error of at most 0.0003.
Values may be sent and summed in bfloat16 or wider, within the bound.
No kernel may reach another device: no remote copies, remote signals or barrier semaphores. Data moves between devices by JAX's collectives and lax.ppermute only.
A program may use at most 64 MiB of HBM per device.

```python
import math
import jax
import jax.numpy as jnp
from jax import lax

D = 256
ROW_DEV = 1024
MOST = 16
ROUNDS = 3
SHARDS = 256
ROWS_ALL = 262144


def draw_points(key, part):
    key = jax.random.fold_in(key, 11)
    member_key, centre_key, noise_key = jax.random.split(key, 3)
    groups = SHARDS * MOST
    spread = 1.0 / math.sqrt(D)
    member = jax.random.randint(member_key, (ROWS_ALL,), 0, groups).astype(jnp.int32)
    ramp = jnp.arange(ROWS_ALL, dtype=jnp.float32) / float(ROWS_ALL - 1)
    centres = jax.random.normal(centre_key, (groups, D), jnp.float32) * spread
    noise = jax.random.normal(noise_key, (ROWS_ALL, D), jnp.float32)
    level = 0.15 + 0.4 * ramp
    rows_out = centres[member] + noise * (level * spread)[:, None]
    return jnp.clip(rows_out, -1.5, 1.5).astype(jnp.bfloat16)


def draw_init_dist(key, part):
    key = jax.random.fold_in(key, 3)
    ramp = jnp.arange(ROWS_ALL, dtype=jnp.float32) / float(ROWS_ALL - 1)
    base = jnp.exp(jax.random.uniform(key, (ROWS_ALL,), jnp.float32, jnp.log(0.5), jnp.log(2.0)))
    return jnp.clip(base * (1.0 + 2.0 * ramp), 0.5, 6.0)


def draw_picks(key, part):
    key = jax.random.fold_in(key, 5)
    chosen = jax.random.randint(key, (ROUNDS, SHARDS * MOST), 0, ROW_DEV)
    return chosen.at[:, 0].set(ROW_DEV - 1).astype(jnp.int32)


def draw_pick_counts(key, part):
    key = jax.random.fold_in(key, 7)
    first_key, second_key = jax.random.split(key)
    counts = jax.random.randint(first_key, (ROUNDS, SHARDS), 1, MOST + 1)
    fullest = jax.random.randint(second_key, (ROUNDS,), 0, SHARDS)
    column = jnp.arange(SHARDS, dtype=jnp.int32)[None, :]
    return jnp.where(column == fullest[:, None], MOST, counts).astype(jnp.int32)


def setup_inputs(seed: int = 0) -> dict:
    splits = jax.random.split(jax.random.key(seed), 5)
    return {
        "points": draw_points(jax.random.fold_in(splits[4], 71), 0),
        "init_dist": draw_init_dist(jax.random.fold_in(splits[4], 71), 0),
        "picks": draw_picks(jax.random.fold_in(splits[4], 71), 0),
        "pick_counts": draw_pick_counts(jax.random.fold_in(splits[4], 71), 0),
    }


def reference(points, init_dist, picks, pick_counts):
    row_sq = jnp.sum(jnp.square(points.astype(jnp.float32)), axis=1)
    blocks = points.reshape(SHARDS, ROW_DEV, D)
    block_sq = row_sq.reshape(SHARDS, ROW_DEV)
    current = init_dist.reshape(SHARDS, ROW_DEV)
    owner = jnp.arange(SHARDS * MOST, dtype=jnp.int32) // MOST
    slot_no = jnp.arange(SHARDS * MOST, dtype=jnp.int32) % MOST
    costs = []
    for step in range(ROUNDS):
        global_idx = (owner * ROW_DEV + picks[step]).astype(jnp.int32)
        cand = points[global_idx]
        live = slot_no < pick_counts[step][owner]
        cand_sq = jnp.where(live, row_sq[global_idx], jnp.inf)

        def one_block(args):
            rows_blk, sq_blk, cur_blk = args
            inner = jnp.dot(rows_blk, cand.T, preferred_element_type=jnp.float32)
            dist = jnp.maximum(sq_blk[:, None] + cand_sq[None, :] - 2.0 * inner, 0.0)
            return jnp.minimum(cur_blk, jnp.min(dist, axis=1))

        current = lax.map(one_block, (blocks, block_sq, current))
        costs.append(jnp.sum(current))
    min_dist = current.reshape(-1)
    normalized = min_dist * float(ROWS_ALL) / costs[-1]
    return min_dist, normalized, jnp.stack(costs)
```

```python
import jax
import jax.numpy as jnp
from jax import lax
from jax.experimental import pallas as pl
from jax.experimental.pallas import tpu as pltpu
from jax.sharding import Mesh, PartitionSpec as P

CHIPS_Z, CHIPS_X, CORES = 8, 4, 2
TILE = 256


def nearest_kernel(first_ref, *refs):
    blocks, (mine_ref, other_ref, out_ref, sq_ref) = refs[:-4], refs[-4:]
    rounds = out_ref.shape[1]
    sources, slots, width = mine_ref.shape
    most = slots // rounds
    halves = (mine_ref, other_ref)
    rows = sources * most

    def half_round(half, step):
        return halves[half][:, step * most : (step + 1) * most, :].reshape(rows, width)

    for half in range(2):
        for step in range(rounds):
            values = half_round(half, step).astype(jnp.float32)
            squares = jnp.sum(values * values, axis=1, keepdims=True)
            sq_ref[half, step] = jnp.broadcast_to(squares, (rows, 128))

    count = len(blocks)
    for shift, block_ref in enumerate(blocks):
        place = lax.rem(first_ref[0] - shift + count, count)

        def one_tile(tile, _, block_ref=block_ref, place=place):
            start = pl.multiple_of(tile * TILE, TILE)
            weights = block_ref[pl.ds(start, TILE), :] * jnp.bfloat16(-2.0)
            for step in range(rounds):
                best = None
                for half in range(2):
                    values = half_round(half, step)
                    for part in range(0, rows, TILE):
                        inner = lax.dot_general(
                            values[part : part + TILE],
                            weights,
                            (((1,), (1,)), ((), ())),
                            preferred_element_type=jnp.float32,
                        )
                        squares = sq_ref[half, step, part : part + TILE, :]
                        dist = inner + jnp.concatenate([squares] * (TILE // 128), axis=1)
                        low = jnp.min(dist.reshape(TILE // 8, 8, TILE), axis=0)
                        best = low if best is None else jnp.minimum(best, low)
                out_ref[place, step : step + 1, pl.ds(start, TILE)] = jnp.min(
                    best, axis=0, keepdims=True
                )
            return 0

        lax.fori_loop(0, block_ref.shape[0] // TILE, one_tile, 0)


def nearest(first, blocks, mine, other, rounds):
    sources, slots, _ = mine.shape
    vmem = pl.BlockSpec(memory_space=pltpu.VMEM)
    return pl.pallas_call(
        nearest_kernel,
        out_shape=jax.ShapeDtypeStruct((len(blocks), rounds, blocks[0].shape[0]), jnp.float32),
        in_specs=[pl.BlockSpec(memory_space=pltpu.SMEM)] + [vmem] * (len(blocks) + 2),
        out_specs=vmem,
        scratch_shapes=[pltpu.VMEM((2, rounds, sources * (slots // rounds), 128), jnp.float32)],
        compiler_params=pltpu.CompilerParams(vmem_limit_bytes=32 * 1024 * 1024),
    )(first, *blocks, mine, other)


def shards(points, init_dist, picks, pick_counts):
    rounds, most = picks.shape
    rows, width = points.shape
    subs = lax.axis_size("y")
    groups = lax.axis_size(("z", "x"))
    blocks = [points] + [
        lax.ppermute(points, "y", [(i, (i + shift) % subs) for i in range(subs)])
        for shift in range(1, subs)
    ]
    slot_no = jnp.arange(most, dtype=jnp.int32)[None, :]
    named = jnp.where(slot_no < pick_counts, picks, picks[:, :1]).reshape(-1)
    select = (named[:, None] == jnp.arange(rows, dtype=jnp.int32)[None, :]).astype(jnp.bfloat16)
    cand = jnp.dot(select, points, preferred_element_type=jnp.float32).astype(jnp.bfloat16)
    mine = lax.all_to_all(
        jnp.broadcast_to(cand[None], (groups,) + cand.shape), ("z", "x"), 0, 0, tiled=True
    )
    other = lax.ppermute(mine, "c", [(0, 1), (1, 0)])
    first = lax.axis_index("y").astype(jnp.int32)[None]
    partial_low = nearest(first, blocks, mine, other, rounds)
    low = jnp.min(lax.all_to_all(partial_low, "y", 0, 0, tiled=True), axis=0)
    row_sq = jnp.sum(jnp.square(points.astype(jnp.float32)), axis=1)
    dist = jnp.maximum(row_sq[None] + low, 0.0)
    current = init_dist
    partials = []
    for step in range(rounds):
        current = jnp.minimum(current, dist[step])
        partials.append(jnp.sum(current))
    everyone = ("z", "x", "c", "y")
    devices = lax.axis_size(everyone)
    shares = jnp.broadcast_to(jnp.stack(partials)[None], (devices, rounds))
    round_costs = jnp.sum(lax.all_to_all(shares, everyone, 0, 0, tiled=True), axis=0)
    normalized = current * float(rows * devices) / round_costs[rounds - 1]
    return (current, normalized, round_costs)


def solution(mesh):
    fine = Mesh(
        mesh.devices.reshape(CHIPS_Z, CHIPS_X, CORES, mesh.shape["sub"]), ("z", "x", "c", "y")
    )
    rows = ("z", "x", "c", "y")
    return jax.shard_map(
        shards,
        mesh=fine,
        in_specs=(P(rows, None), P(rows), P(None, rows), P(None, rows)),
        out_specs=(P(rows), P(rows), P()),
        check_vma=False,
    )
```

```python
import jax
import jax.numpy as jnp
from jax import lax
from jax.experimental import pallas as pl
from jax.experimental.pallas import tpu as pltpu
from jax.sharding import Mesh, PartitionSpec as P

CHIPS_Z, CHIPS_X, CORES = 8, 4, 2
PART = 256
LANES = 128
TURN_FLOPS = 3_000_000
F32, BF16 = jnp.float32, jnp.bfloat16
VMEM = pl.BlockSpec(memory_space=pltpu.VMEM)
SMEM = pl.BlockSpec(memory_space=pltpu.SMEM)
PARAMS = pltpu.CompilerParams(vmem_limit_bytes=40 * 1024 * 1024)


def pick_kernel(picks_ref, counts_ref, points_ref, out_ref, select_ref):
    rounds, most = picks_ref.shape
    column = lax.broadcasted_iota(jnp.int32, (1, points_ref.shape[0]), 1)
    for step in range(rounds):
        for slot in range(most):
            named = jnp.where(slot < counts_ref[step], picks_ref[step, slot], picks_ref[step, 0])
            row = step * most + slot
            select_ref[row : row + 1, :] = jnp.where(column == named, 1.0, 0.0).astype(F32)
    cand = jnp.dot(
        select_ref[...].astype(BF16), points_ref[...], preferred_element_type=F32
    ).astype(BF16)
    for copy in range(out_ref.shape[0]):
        out_ref[copy] = cand


def pick_rows(picks, counts, points, copies):
    slots = picks.shape[0] * picks.shape[1]
    rows, width = points.shape
    return pl.pallas_call(
        pick_kernel,
        out_shape=jax.ShapeDtypeStruct((copies, slots, width), BF16),
        in_specs=[SMEM, SMEM, VMEM],
        out_specs=VMEM,
        scratch_shapes=[pltpu.VMEM((slots, rows), F32)],
        compiler_params=PARAMS,
        cost_estimate=pl.CostEstimate(
            flops=2 * slots * rows * width, bytes_accessed=rows * width * 2, transcendentals=0
        ),
    )(picks, counts, points)


def turn_kernel(place_ref, *refs):
    blocks, (turned_ref, length_ref) = refs[:-2], refs[-2:]
    for number, block_ref in enumerate(blocks):
        turned = (block_ref[...] * BF16(-2.0)).T
        place = place_ref[number]
        turned_ref[place] = turned
        wide = turned.astype(F32)
        length_ref[place] = jnp.sum(wide * wide, axis=0, keepdims=True) * 0.25


def turn(places, blocks):
    count, (rows, width) = len(blocks), blocks[0].shape
    return pl.pallas_call(
        turn_kernel,
        out_shape=(
            jax.ShapeDtypeStruct((count, width, rows), BF16),
            jax.ShapeDtypeStruct((count, 1, rows), F32),
        ),
        in_specs=[SMEM] + [VMEM] * count,
        out_specs=(VMEM, VMEM),
        compiler_params=PARAMS,
        cost_estimate=pl.CostEstimate(
            flops=TURN_FLOPS, bytes_accessed=count * rows * width * 4, transcendentals=0
        ),
    )(places, *blocks)


def near_body(turned_ref, cand_ref, sq_ref, number, step, rounds):
    sources, slots, width = cand_ref.shape
    most = slots // rounds
    rows = sources * most
    count = turned_ref.shape[2]
    values = cand_ref[:, step * most : (step + 1) * most, :].reshape(rows, width)
    weights = turned_ref[number]
    best = None
    for part in range(0, rows, PART):
        inner = jnp.dot(values[part : part + PART], weights, preferred_element_type=F32)
        squares = sq_ref[step, part : part + PART, :]
        dist = inner + jnp.concatenate([squares] * (count // LANES), axis=1)
        low = jnp.min(dist.reshape(PART // 8, 8, count), axis=0)
        best = low if best is None else jnp.minimum(best, low)
    return jnp.min(best, axis=0, keepdims=True)


def squares_of(cand_ref, sq_ref, rounds):
    sources, slots, width = cand_ref.shape
    most = slots // rounds
    rows = sources * most
    for step in range(rounds):
        values = cand_ref[:, step * most : (step + 1) * most, :].reshape(rows, width).astype(F32)
        squares = jnp.sum(values * values, axis=1, keepdims=True)
        sq_ref[step] = jnp.broadcast_to(squares, (rows, LANES))


def first_kernel(turned_ref, cand_ref, out_ref, sq_ref):
    rounds = out_ref.shape[1]
    squares_of(cand_ref, sq_ref, rounds)
    for number in range(turned_ref.shape[0]):
        for step in range(rounds):
            out_ref[number, step : step + 1, :] = near_body(
                turned_ref, cand_ref, sq_ref, number, step, rounds
            )


def second_kernel(place_ref, turned_ref, cand_ref, low_ref, length_ref, init_ref, out_ref, sq_ref):
    copies, count, rounds, _ = out_ref.shape
    squares_of(cand_ref, sq_ref, rounds)
    mine = place_ref[0]
    for number in range(count):
        limit = jnp.where(mine == number, init_ref[...], jnp.inf)
        for step in range(rounds):
            low = near_body(turned_ref, cand_ref, sq_ref, number, step, rounds)
            low = jnp.minimum(low, low_ref[number, step : step + 1, :])
            dist = jnp.minimum(jnp.maximum(low + length_ref[number], 0.0), limit)
            for copy in range(copies):
                out_ref[copy, number, step : step + 1, :] = dist


def cost_of(turned, cand):
    count, width, rows = turned.shape
    return pl.CostEstimate(
        flops=2 * count * rows * width * cand.shape[0] * cand.shape[1],
        bytes_accessed=2 * (turned.size + cand.size),
        transcendentals=0,
    )


def first_half(turned, cand, rounds):
    count, width, rows = turned.shape
    return pl.pallas_call(
        first_kernel,
        out_shape=jax.ShapeDtypeStruct((count, rounds, rows), F32),
        in_specs=[VMEM] * 2,
        out_specs=VMEM,
        scratch_shapes=[pltpu.VMEM((rounds, cand.shape[0] * cand.shape[1] // rounds, LANES), F32)],
        compiler_params=PARAMS,
        cost_estimate=cost_of(turned, cand),
    )(turned, cand)


def second_half(places, turned, cand, low, lengths, init_row, rounds):
    count, width, rows = turned.shape
    return pl.pallas_call(
        second_kernel,
        out_shape=jax.ShapeDtypeStruct((count, count, rounds, rows), F32),
        in_specs=[SMEM] + [VMEM] * 5,
        out_specs=VMEM,
        scratch_shapes=[pltpu.VMEM((rounds, cand.shape[0] * cand.shape[1] // rounds, LANES), F32)],
        compiler_params=PARAMS,
        cost_estimate=cost_of(turned, cand),
    )(places, turned, cand, low, lengths, init_row)


def total_kernel(place_ref, dist_ref, own_ref, total_ref):
    rounds = dist_ref.shape[2]
    dist = jnp.min(dist_ref[...], axis=0)
    lane = lax.broadcasted_iota(jnp.int32, total_ref.shape, 1)
    total = jnp.zeros(total_ref.shape, F32)
    current = None
    for step in range(rounds):
        current = dist[:, step, :] if step == 0 else jnp.minimum(current, dist[:, step, :])
        total = jnp.where(lane == step, jnp.sum(current), total)
    total_ref[...] = total
    mine = place_ref[0]
    own = current[0:1]
    for number in range(1, current.shape[0]):
        own = jnp.where(mine == number, current[number : number + 1], own)
    own_ref[...] = own


def totals(places, dist, peers):
    return pl.pallas_call(
        total_kernel,
        out_shape=(
            jax.ShapeDtypeStruct((1, dist.shape[3]), F32),
            jax.ShapeDtypeStruct((peers, LANES), F32),
        ),
        in_specs=[SMEM, VMEM],
        out_specs=(VMEM, VMEM),
        compiler_params=PARAMS,
    )(places, dist)


def finish_kernel(all_rows, own_ref, share_ref, normal_ref, cost_ref):
    rounds = cost_ref.shape[1]
    total = jnp.sum(share_ref[...], axis=0, keepdims=True)
    cost_ref[...] = total[:, :rounds]
    normal_ref[...] = own_ref[...] * all_rows / total[:, rounds - 1 : rounds]


def finish(own, shares, rounds, all_rows):
    def body(*refs):
        finish_kernel(all_rows, *refs)

    return pl.pallas_call(
        body,
        out_shape=(
            jax.ShapeDtypeStruct(own.shape, F32),
            jax.ShapeDtypeStruct((1, rounds), F32),
        ),
        in_specs=[VMEM, VMEM],
        out_specs=(VMEM, VMEM),
        compiler_params=PARAMS,
    )(own, shares)


def shards(points, init_dist, picks, pick_counts):
    rounds, most = picks.shape
    rows, width = points.shape
    subs = lax.axis_size("y")
    sub = lax.axis_index("y").astype(jnp.int32)
    blocks = [points] + [
        lax.ppermute(points, "y", [(i, (i + shift) % subs) for i in range(subs)])
        for shift in range(1, subs)
    ]
    places = (sub - jnp.arange(subs, dtype=jnp.int32)) % subs
    cand = pick_rows(picks, pick_counts.reshape(-1), points, CHIPS_Z)
    along_z = lax.all_to_all(cand, "z", 0, 0, tiled=True)
    along_z, blocks[1], blocks[3] = lax.optimization_barrier((along_z, blocks[1], blocks[3]))
    mine = lax.all_to_all(
        jnp.broadcast_to(along_z[None], (CHIPS_X,) + along_z.shape), "x", 0, 0
    ).reshape((CHIPS_Z * CHIPS_X,) + cand.shape[1:])
    other = lax.ppermute(mine, "c", [(0, 1), (1, 0)])
    turned, lengths = turn(places, blocks)
    low = first_half(turned, mine, rounds)
    dist = second_half(places, turned, other, low, lengths, init_dist[None], rounds)
    shared = lax.all_to_all(dist, "y", 0, 0, tiled=True)
    peers = ("z", "x", "c")
    own, total = totals(places, shared, lax.axis_size(("z", "x")))
    total = total + lax.ppermute(total, "c", [(0, 1), (1, 0)])
    shares = lax.all_to_all(total, ("z", "x"), 0, 0, tiled=True)
    all_rows = float(rows * subs * lax.axis_size(peers))
    normalized, round_costs = finish(own, shares, rounds, all_rows)
    return (own[0], normalized[0], round_costs[0])


def solution(mesh):
    fine = Mesh(
        mesh.devices.reshape(CHIPS_Z, CHIPS_X, CORES, mesh.shape["sub"]), ("z", "x", "c", "y")
    )
    rows = ("z", "x", "c", "y")
    return jax.shard_map(
        shards,
        mesh=fine,
        in_specs=(P(rows, None), P(rows), P(None, rows), P(None, rows)),
        out_specs=(P(rows), P(rows), P()),
        check_vma=False,
    )
```

```python
import jax
import jax.numpy as jnp
from jax import lax
from jax.experimental import pallas as pl
from jax.experimental.pallas import tpu as pltpu
from jax.sharding import Mesh, PartitionSpec as P

CHIPS_Z, CHIPS_X, CORES = 8, 4, 2
PART = 256
LANES = 128
F32, BF16 = jnp.float32, jnp.bfloat16
VMEM = pl.BlockSpec(memory_space=pltpu.VMEM)
ANY = pl.BlockSpec(memory_space=pl.ANY)
SMEM = pl.BlockSpec(memory_space=pltpu.SMEM)
PARAMS = pltpu.CompilerParams(vmem_limit_bytes=40 * 1024 * 1024)


def pick_kernel(picks_hbm, counts_hbm, points_hbm, out_ref, picks_ref, counts_ref, points_ref, select_ref, sems):
    copies = [
        pltpu.make_async_copy(points_hbm, points_ref, sems.at[0]),
        pltpu.make_async_copy(picks_hbm, picks_ref, sems.at[1]),
        pltpu.make_async_copy(counts_hbm, counts_ref, sems.at[2]),
    ]
    for copy in copies:
        copy.start()
    copies[1].wait()
    copies[2].wait()
    rounds, most = picks_ref.shape
    column = lax.broadcasted_iota(jnp.int32, (1, points_ref.shape[0]), 1)
    for step in range(rounds):
        for slot in range(most):
            named = jnp.where(slot < counts_ref[step], picks_ref[step, slot], picks_ref[step, 0])
            row = step * most + slot
            select_ref[row : row + 1, :] = jnp.where(column == named, 1.0, 0.0).astype(F32)
    select = select_ref[...].astype(BF16)
    copies[0].wait()
    cand = jnp.dot(select, points_ref[...], preferred_element_type=F32).astype(BF16)
    for place in range(out_ref.shape[0]):
        out_ref[place] = cand


def pick_rows(picks, counts, points, copies):
    slots = picks.shape[0] * picks.shape[1]
    rows, width = points.shape
    return pl.pallas_call(
        pick_kernel,
        out_shape=jax.ShapeDtypeStruct((copies, slots, width), BF16),
        in_specs=[ANY, ANY, ANY],
        out_specs=VMEM,
        scratch_shapes=[
            pltpu.SMEM(picks.shape, jnp.int32),
            pltpu.SMEM(counts.shape, jnp.int32),
            pltpu.VMEM(points.shape, BF16),
            pltpu.VMEM((slots, rows), F32),
            pltpu.SemaphoreType.DMA((3,)),
        ],
        compiler_params=pltpu.CompilerParams(vmem_limit_bytes=60 * 1024 * 1024),
        cost_estimate=pl.CostEstimate(
            flops=2 * slots * rows * width, bytes_accessed=rows * width * 2, transcendentals=0
        ),
    )(picks, counts, points)


def turn_kernel(*refs):
    blocks, (turned_ref, length_ref) = refs[:-2], refs[-2:]
    width = turned_ref.shape[1]
    place = 0
    for block_ref in blocks:
        rows = block_ref.shape[0]
        number, start = divmod(place, turned_ref.shape[2])
        turned = (block_ref[...] * BF16(-2.0)).T
        turned_ref[number, :, start : start + rows] = turned
        wide = turned.astype(F32)
        length_ref[number, :, start : start + rows] = jnp.sum(wide * wide, axis=0, keepdims=True) * 0.25
        place += rows


def turn(blocks, rows):
    width = blocks[0].shape[1]
    count = sum(block.shape[0] for block in blocks) // rows
    return pl.pallas_call(
        turn_kernel,
        out_shape=(
            jax.ShapeDtypeStruct((count, width, rows), BF16),
            jax.ShapeDtypeStruct((count, 1, rows), F32),
        ),
        in_specs=[VMEM] * len(blocks),
        out_specs=(VMEM, VMEM),
        compiler_params=PARAMS,
        cost_estimate=pl.CostEstimate(
            flops=count * rows * width * 3, bytes_accessed=count * rows * width * 4, transcendentals=0
        ),
    )(*blocks)


def half_round(cand_ref, step, rounds):
    sources, slots, width = cand_ref.shape
    most = slots // rounds
    return cand_ref[:, step * most : (step + 1) * most, :].reshape(sources * most, width)


def squares_of(cands, sq_ref, rounds):
    for step in range(rounds):
        base = 0
        for cand_ref in cands:
            values = half_round(cand_ref, step, rounds).astype(F32)
            squares = jnp.sum(values * values, axis=1, keepdims=True)
            rows = values.shape[0]
            sq_ref[step, base : base + rows] = jnp.broadcast_to(squares, (rows, LANES))
            base += rows


def lowest(weights, cands, sq_ref, step, rounds):
    count = weights.shape[1]
    best = None
    base = 0
    for cand_ref in cands:
        values = half_round(cand_ref, step, rounds)
        for part in range(0, values.shape[0], PART):
            piece = values[part : part + PART]
            size = piece.shape[0]
            inner = jnp.dot(piece, weights, preferred_element_type=F32)
            squares = sq_ref[step, base : base + size, :]
            dist = inner + jnp.concatenate([squares] * (count // LANES), axis=1)
            low = jnp.min(dist.reshape(size // 8, 8, count), axis=0)
            best = low if best is None else jnp.minimum(best, low)
            base += size
    return jnp.min(best, axis=0, keepdims=True)


def blocks_of(turned):
    return [(ref, number) for ref in turned for number in range(ref.shape[0])]


def near_cost(turned, cands):
    columns = sum(block.shape[0] * block.shape[2] for block in turned)
    return pl.CostEstimate(
        flops=2 * columns * sum(cand.size for cand in cands),
        bytes_accessed=2 * sum(x.size for x in turned + cands),
        transcendentals=0,
    )


def near(turned, cands, low, rounds):
    count, rows = sum(block.shape[0] for block in turned), turned[0].shape[2]

    def body(*refs):
        turned_refs, refs = refs[: len(turned)], refs[len(turned) :]
        cand_refs, refs = refs[: len(cands)], refs[len(cands) :]
        out_ref, sq_ref = refs[-2:]
        squares_of(cand_refs, sq_ref, rounds)
        for place, (ref, number) in enumerate(blocks_of(turned_refs)):
            for step in range(rounds):
                value = lowest(ref[number], cand_refs, sq_ref, step, rounds)
                if low is not None:
                    value = jnp.minimum(value, refs[0][place, step : step + 1, :])
                out_ref[place, step : step + 1, :] = value

    extra = [] if low is None else [low]
    slots = sum(cand.shape[0] * cand.shape[1] for cand in cands)
    return pl.pallas_call(
        body,
        out_shape=jax.ShapeDtypeStruct((count, rounds, rows), F32),
        in_specs=[VMEM] * (len(turned) + len(cands) + len(extra)),
        out_specs=VMEM,
        scratch_shapes=[pltpu.VMEM((rounds, slots // rounds, LANES), F32)],
        compiler_params=PARAMS,
        cost_estimate=near_cost(turned, cands),
    )(*turned, *cands, *extra)


def last_near(places, turned, cands, low, lengths, init_row, rounds):
    count, rows = sum(block.shape[0] for block in turned), turned[0].shape[2]

    def body(place_ref, *refs):
        turned_refs, refs = refs[: len(turned)], refs[len(turned) :]
        length_refs, refs = refs[: len(turned)], refs[len(turned) :]
        cand_refs, refs = refs[: len(cands)], refs[len(cands) :]
        low_ref, init_ref, out_ref, sq_ref = refs
        squares_of(cand_refs, sq_ref, rounds)
        blocks = zip(blocks_of(turned_refs), blocks_of(length_refs))
        for number, ((ref, inner), (length_ref, _)) in enumerate(blocks):
            place = place_ref[number]
            for step in range(rounds):
                value = lowest(ref[inner], cand_refs, sq_ref, step, rounds)
                value = jnp.minimum(value, low_ref[number, step : step + 1, :])
                dist = jnp.maximum(value + length_ref[inner], 0.0)
                if number == 0:
                    dist = jnp.minimum(dist, init_ref[...])
                for copy in range(out_ref.shape[0]):
                    out_ref[copy, step, pl.ds(place, 1), :] = dist

    slots = sum(cand.shape[0] * cand.shape[1] for cand in cands)
    return pl.pallas_call(
        body,
        out_shape=jax.ShapeDtypeStruct((count, rounds, count, rows), F32),
        in_specs=[SMEM] + [VMEM] * (len(turned) + len(lengths) + len(cands) + 2),
        out_specs=VMEM,
        scratch_shapes=[pltpu.VMEM((rounds, slots // rounds, LANES), F32)],
        compiler_params=PARAMS,
        cost_estimate=near_cost(turned, cands),
    )(places, *turned, *lengths, *cands, low, init_row)


def total_kernel(place_ref, dist_ref, own_ref, total_ref):
    rounds = dist_ref.shape[1]
    lane = lax.broadcasted_iota(jnp.int32, total_ref.shape, 1)
    total = jnp.zeros(total_ref.shape, F32)
    current = None
    for step in range(rounds):
        dist = jnp.min(dist_ref[:, step], axis=0)
        current = dist if step == 0 else jnp.minimum(current, dist)
        total = jnp.where(lane == step, jnp.sum(current), total)
    total_ref[...] = total
    mine = place_ref[0]
    own = current[0:1]
    for number in range(1, current.shape[0]):
        own = jnp.where(mine == number, current[number : number + 1], own)
    own_ref[...] = own


def totals(places, dist, peers):
    return pl.pallas_call(
        total_kernel,
        out_shape=(
            jax.ShapeDtypeStruct((1, dist.shape[3]), F32),
            jax.ShapeDtypeStruct((peers, LANES), F32),
        ),
        in_specs=[SMEM, VMEM],
        out_specs=(VMEM, VMEM),
        compiler_params=PARAMS,
    )(places, dist)


def finish(own, shares, rounds, all_rows):
    def body(own_ref, share_ref, min_ref, normal_ref, cost_ref):
        total = jnp.sum(share_ref[...], axis=0, keepdims=True)
        cost_ref[...] = total[:, :rounds]
        min_ref[...] = own_ref[...]
        normal_ref[...] = own_ref[...] * all_rows / total[:, rounds - 1 : rounds]

    row = jax.ShapeDtypeStruct(own.shape, F32)
    return pl.pallas_call(
        body,
        out_shape=(row, row, jax.ShapeDtypeStruct((1, rounds), F32)),
        in_specs=[VMEM, VMEM],
        out_specs=(VMEM, VMEM, VMEM),
        compiler_params=PARAMS,
    )(own, shares)


def shift(block, axis, size, by):
    return lax.ppermute(block, axis, [(i, (i + by) % size) for i in range(size)])


def shards(points, init_dist, picks, pick_counts):
    rounds, most = picks.shape
    rows, width = points.shape
    subs = lax.axis_size("y")
    sub = lax.axis_index("y").astype(jnp.int32)
    half = rows // 2
    behind, ahead = (shift(points, "y", subs, by) for by in (1, 3))
    across = [shift(behind[:half], "y", subs, 1), shift(ahead[half:], "y", subs, 3)]
    places = (sub + jnp.array([0, 3, 1, 2], jnp.int32)) % subs
    cand = pick_rows(picks, pick_counts.reshape(-1), points, CHIPS_Z)
    along_z = lax.all_to_all(cand, "z", 0, 0, tiled=True)
    from_x = [shift(along_z, "x", CHIPS_X, by) for by in (2, 1, 3)]
    opposite, after, before = from_x
    swapped = shift(along_z, "c", CORES, 1)
    near_turned, near_lengths = turn([points, behind, ahead], rows)
    far_turned, far_lengths = turn(across, rows)
    turned, lengths = [near_turned, far_turned], [near_lengths, far_lengths]
    low = near(turned, [along_z, swapped], None, rounds)
    beside = [shift(piece, "c", CORES, 1) for piece in (after, before)]
    low = near(turned, [after, before], low, rounds)
    low = near(turned, beside, low, rounds)
    opposite, low = lax.optimization_barrier((opposite, low))
    last = shift(opposite, "c", CORES, 1)
    low = near(turned, [opposite], low, rounds)
    last = [last]
    dist = last_near(places, turned, last, low, lengths, init_dist[None], rounds)
    shared = lax.all_to_all(dist, "y", 0, 0, tiled=True)
    own, total = totals(places, shared, lax.axis_size(("z", "x")))
    total = total + shift(total, "c", CORES, 1)
    shares = lax.all_to_all(total, ("z", "x"), 0, 0, tiled=True)
    all_rows = float(rows * lax.axis_size(("z", "x", "c", "y")))
    min_dist, normalized, round_costs = finish(own, shares, rounds, all_rows)
    return (min_dist[0], normalized[0], round_costs[0])


def solution(mesh):
    fine = Mesh(
        mesh.devices.reshape(CHIPS_Z, CHIPS_X, CORES, mesh.shape["sub"]), ("z", "x", "c", "y")
    )
    rows = ("z", "x", "c", "y")
    return jax.shard_map(
        shards,
        mesh=fine,
        in_specs=(P(rows, None), P(rows), P(None, rows), P(None, rows)),
        out_specs=(P(rows), P(rows), P()),
        check_vma=False,
    )
```

```python
import jax
import jax.numpy as jnp
from jax import lax
from jax.experimental import pallas as pl
from jax.experimental.pallas import tpu as pltpu
from jax.sharding import Mesh, PartitionSpec as P

CHIPS_Z, CHIPS_X, CORES = 8, 4, 2
PART = 256
LANES = 128
F32, BF16 = jnp.float32, jnp.bfloat16
VMEM = pl.BlockSpec(memory_space=pltpu.VMEM)
ANY = pl.BlockSpec(memory_space=pl.ANY)
SMEM = pl.BlockSpec(memory_space=pltpu.SMEM)
PARAMS = pltpu.CompilerParams(vmem_limit_bytes=40 * 1024 * 1024)


def pick_kernel(picks_hbm, counts_hbm, points_hbm, out_ref, picks_ref, counts_ref, points_ref, sems):
    copies = [
        pltpu.make_async_copy(picks_hbm, picks_ref, sems.at[0]),
        pltpu.make_async_copy(counts_hbm, counts_ref, sems.at[1]),
        pltpu.make_async_copy(points_hbm, points_ref, sems.at[2]),
    ]
    for copy in copies:
        copy.start()
    rounds, most = picks_ref.shape
    rows = points_ref.shape[0]
    slot = lax.broadcasted_iota(jnp.int32, (1, most), 1)
    diagonal = lax.broadcasted_iota(jnp.int32, (most, most), 0) == lax.broadcasted_iota(
        jnp.int32, (most, most), 1
    )
    column = lax.broadcasted_iota(jnp.int32, (most, rows), 1)
    copies[0].wait()
    copies[1].wait()
    select = []
    for step in range(rounds):
        picked = picks_ref[step : step + 1, :]
        named = jnp.where(slot < counts_ref[step], picked, picked[:, :1])
        down = jnp.sum(jnp.where(diagonal, named, 0), axis=1, keepdims=True)
        select.append(jnp.where(column == down, 1.0, 0.0).astype(BF16))
    select = jnp.concatenate(select, axis=0)
    copies[2].wait()
    cand = jnp.dot(select, points_ref[...], preferred_element_type=F32).astype(BF16)
    for place in range(out_ref.shape[0]):
        out_ref[place] = cand


def pick_rows(picks, counts, points, copies):
    slots = picks.shape[0] * picks.shape[1]
    rows, width = points.shape
    return pl.pallas_call(
        pick_kernel,
        out_shape=jax.ShapeDtypeStruct((copies, slots, width), BF16),
        in_specs=[ANY, ANY, ANY],
        out_specs=VMEM,
        scratch_shapes=[
            pltpu.VMEM(picks.shape, jnp.int32),
            pltpu.SMEM(counts.shape, jnp.int32),
            pltpu.VMEM(points.shape, BF16),
            pltpu.SemaphoreType.DMA((3,)),
        ],
        compiler_params=pltpu.CompilerParams(vmem_limit_bytes=60 * 1024 * 1024),
        cost_estimate=pl.CostEstimate(
            flops=2 * slots * rows * width, bytes_accessed=rows * width * 2, transcendentals=0
        ),
    )(picks, counts, points)


def turn_kernel(*refs):
    blocks, (turned_ref, length_ref) = refs[:-2], refs[-2:]
    width = turned_ref.shape[1]
    place = 0
    for block_ref in blocks:
        rows = block_ref.shape[0]
        number, start = divmod(place, turned_ref.shape[2])
        turned = (block_ref[...] * BF16(-2.0)).T
        turned_ref[number, :, start : start + rows] = turned
        wide = turned.astype(F32)
        length_ref[number, :, start : start + rows] = jnp.sum(wide * wide, axis=0, keepdims=True) * 0.25
        place += rows


def turn(blocks, rows):
    width = blocks[0].shape[1]
    count = sum(block.shape[0] for block in blocks) // rows
    return pl.pallas_call(
        turn_kernel,
        out_shape=(
            jax.ShapeDtypeStruct((count, width, rows), BF16),
            jax.ShapeDtypeStruct((count, 1, rows), F32),
        ),
        in_specs=[VMEM] * len(blocks),
        out_specs=(VMEM, VMEM),
        compiler_params=PARAMS,
        cost_estimate=pl.CostEstimate(
            flops=count * rows * width * 3, bytes_accessed=count * rows * width * 4, transcendentals=0
        ),
    )(*blocks)


def half_round(cand_ref, step, rounds):
    sources, slots, width = cand_ref.shape
    most = slots // rounds
    return cand_ref[:, step * most : (step + 1) * most, :].reshape(sources * most, width)


def squares_of(cands, sq_ref, rounds):
    for step in range(rounds):
        base = 0
        for cand_ref in cands:
            values = half_round(cand_ref, step, rounds).astype(F32)
            squares = jnp.sum(values * values, axis=1, keepdims=True)
            rows = values.shape[0]
            sq_ref[step, base : base + rows] = jnp.broadcast_to(squares, (rows, LANES))
            base += rows


def lowest(weights, cands, sq_ref, step, rounds):
    count = weights.shape[1]
    best = None
    base = 0
    for cand_ref in cands:
        values = half_round(cand_ref, step, rounds)
        for part in range(0, values.shape[0], PART):
            piece = values[part : part + PART]
            size = piece.shape[0]
            inner = jnp.dot(piece, weights, preferred_element_type=F32)
            squares = sq_ref[step, base : base + size, :]
            dist = inner + jnp.concatenate([squares] * (count // LANES), axis=1)
            low = jnp.min(dist.reshape(size // 8, 8, count), axis=0)
            best = low if best is None else jnp.minimum(best, low)
            base += size
    return jnp.min(best, axis=0, keepdims=True)


def blocks_of(turned):
    return [(ref, number) for ref in turned for number in range(ref.shape[0])]


def near_cost(turned, cands):
    columns = sum(block.shape[0] * block.shape[2] for block in turned)
    return pl.CostEstimate(
        flops=2 * columns * sum(cand.size for cand in cands),
        bytes_accessed=2 * sum(x.size for x in turned + cands),
        transcendentals=0,
    )


def near(turned, cands, low, rounds):
    count, rows = sum(block.shape[0] for block in turned), turned[0].shape[2]

    def body(*refs):
        turned_refs, refs = refs[: len(turned)], refs[len(turned) :]
        cand_refs, refs = refs[: len(cands)], refs[len(cands) :]
        out_ref, sq_ref = refs[-2:]
        squares_of(cand_refs, sq_ref, rounds)
        for place, (ref, number) in enumerate(blocks_of(turned_refs)):
            for step in range(rounds):
                value = lowest(ref[number], cand_refs, sq_ref, step, rounds)
                if low is not None:
                    value = jnp.minimum(value, refs[0][place, step : step + 1, :])
                out_ref[place, step : step + 1, :] = value

    extra = [] if low is None else [low]
    slots = sum(cand.shape[0] * cand.shape[1] for cand in cands)
    return pl.pallas_call(
        body,
        out_shape=jax.ShapeDtypeStruct((count, rounds, rows), F32),
        in_specs=[VMEM] * (len(turned) + len(cands) + len(extra)),
        out_specs=VMEM,
        scratch_shapes=[pltpu.VMEM((rounds, slots // rounds, LANES), F32)],
        compiler_params=PARAMS,
        cost_estimate=near_cost(turned, cands),
    )(*turned, *cands, *extra)


def last_near(places, turned, cands, low, lengths, init_row, rounds):
    count, rows = sum(block.shape[0] for block in turned), turned[0].shape[2]

    def body(place_ref, *refs):
        turned_refs, refs = refs[: len(turned)], refs[len(turned) :]
        length_refs, refs = refs[: len(turned)], refs[len(turned) :]
        cand_refs, refs = refs[: len(cands)], refs[len(cands) :]
        low_ref, init_ref, out_ref, sq_ref = refs
        squares_of(cand_refs, sq_ref, rounds)
        blocks = zip(blocks_of(turned_refs), blocks_of(length_refs))
        for number, ((ref, inner), (length_ref, _)) in enumerate(blocks):
            place = place_ref[number]
            for step in range(rounds):
                value = lowest(ref[inner], cand_refs, sq_ref, step, rounds)
                value = jnp.minimum(value, low_ref[number, step : step + 1, :])
                dist = jnp.maximum(value + length_ref[inner], 0.0)
                if number == 0:
                    dist = jnp.minimum(dist, init_ref[...])
                out_ref[step, pl.ds(place, 1), :] = dist

    slots = sum(cand.shape[0] * cand.shape[1] for cand in cands)
    return pl.pallas_call(
        body,
        out_shape=jax.ShapeDtypeStruct((rounds, count, rows), F32),
        in_specs=[SMEM] + [VMEM] * (len(turned) + len(lengths) + len(cands) + 2),
        out_specs=VMEM,
        scratch_shapes=[pltpu.VMEM((rounds, slots // rounds, LANES), F32)],
        compiler_params=PARAMS,
        cost_estimate=near_cost(turned, cands),
    )(places, *turned, *lengths, *cands, low, init_row)


def total_kernel(place_ref, *refs):
    dists, (own_ref, total_ref) = refs[:-2], refs[-2:]
    rounds = dists[0].shape[0]
    lane = lax.broadcasted_iota(jnp.int32, total_ref.shape, 1)
    total = jnp.zeros(total_ref.shape, F32)
    current = None
    for step in range(rounds):
        dist = dists[0][step]
        for dist_ref in dists[1:]:
            dist = jnp.minimum(dist, dist_ref[step])
        current = dist if step == 0 else jnp.minimum(current, dist)
        total = jnp.where(lane == step, jnp.sum(current), total)
    total_ref[...] = total
    mine = place_ref[0]
    own = current[0:1]
    for number in range(1, current.shape[0]):
        own = jnp.where(mine == number, current[number : number + 1], own)
    own_ref[...] = own


def totals(places, dists, peers):
    return pl.pallas_call(
        total_kernel,
        out_shape=(
            jax.ShapeDtypeStruct((1, dists[0].shape[2]), F32),
            jax.ShapeDtypeStruct((peers, LANES), F32),
        ),
        in_specs=[SMEM] + [VMEM] * len(dists),
        out_specs=(VMEM, VMEM),
        compiler_params=PARAMS,
    )(places, *dists)


def finish(own, shares, rounds, all_rows):
    def body(own_ref, share_ref, min_ref, normal_ref, cost_ref):
        total = jnp.sum(share_ref[...], axis=0, keepdims=True)
        cost_ref[...] = total[:, :rounds]
        min_ref[...] = own_ref[...]
        normal_ref[...] = own_ref[...] * all_rows / total[:, rounds - 1 : rounds]

    row = jax.ShapeDtypeStruct(own.shape, F32)
    return pl.pallas_call(
        body,
        out_shape=(row, row, jax.ShapeDtypeStruct((1, rounds), F32)),
        in_specs=[VMEM, VMEM],
        out_specs=(VMEM, VMEM, VMEM),
        compiler_params=PARAMS,
    )(own, shares)


def shift(block, axis, size, by):
    return lax.ppermute(block, axis, [(i, (i + by) % size) for i in range(size)])


def shards(points, init_dist, picks, pick_counts):
    rounds, most = picks.shape
    rows, width = points.shape
    subs = lax.axis_size("y")
    sub = lax.axis_index("y").astype(jnp.int32)
    half = rows // 2
    behind, ahead = (shift(points, "y", subs, by) for by in (1, 3))
    across = [shift(behind[:half], "y", subs, 1), shift(ahead[half:], "y", subs, 3)]
    places = (sub + jnp.array([0, 3, 1, 2], jnp.int32)) % subs
    cand = pick_rows(picks, pick_counts.reshape(-1), points, CHIPS_Z)
    along_z = lax.all_to_all(cand, "z", 0, 0, tiled=True)
    from_x = [shift(along_z, "x", CHIPS_X, by) for by in (2, 1, 3)]
    opposite, after, before = from_x
    swapped = shift(along_z, "c", CORES, 1)
    near_turned, near_lengths = turn([points, behind, ahead], rows)
    far_turned, far_lengths = turn(across, rows)
    turned, lengths = [near_turned, far_turned], [near_lengths, far_lengths]
    low = near(turned, [along_z, swapped], None, rounds)
    beside = [shift(piece, "c", CORES, 1) for piece in (after, before)]
    low = near(turned, [after, before], low, rounds)
    low = near(turned, beside, low, rounds)
    opposite, low = lax.optimization_barrier((opposite, low))
    last = shift(opposite, "c", CORES, 1)
    low = near(turned, [opposite], low, rounds)
    last = [last]
    dist = last_near(places, turned, last, low, lengths, init_dist[None], rounds)
    shared = [dist] + [shift(dist, "y", subs, by) for by in (2, 1, 3)]
    own, total = totals(places, shared, lax.axis_size(("z", "x")))
    total = total + shift(total, "c", CORES, 1)
    shares = lax.all_to_all(total, ("z", "x"), 0, 0, tiled=True)
    all_rows = float(rows * lax.axis_size(("z", "x", "c", "y")))
    min_dist, normalized, round_costs = finish(own, shares, rounds, all_rows)
    return (min_dist[0], normalized[0], round_costs[0])


def solution(mesh):
    fine = Mesh(
        mesh.devices.reshape(CHIPS_Z, CHIPS_X, CORES, mesh.shape["sub"]), ("z", "x", "c", "y")
    )
    rows = ("z", "x", "c", "y")
    return jax.shard_map(
        shards,
        mesh=fine,
        in_specs=(P(rows, None), P(rows), P(None, rows), P(None, rows)),
        out_specs=(P(rows), P(rows), P()),
        check_vma=False,
    )
```

```python
import jax
import jax.numpy as jnp
from jax import lax
from jax.experimental import pallas as pl
from jax.experimental.pallas import tpu as pltpu
from jax.sharding import Mesh, PartitionSpec as P

CHIPS_Z, CHIPS_X, CORES = 8, 4, 2
PART = 256
LANES = 128
PLACES = (0, 3, 1, 2)
F32, BF16 = jnp.float32, jnp.bfloat16
VMEM = pl.BlockSpec(memory_space=pltpu.VMEM)
ANY = pl.BlockSpec(memory_space=pl.ANY)
SMEM = pl.BlockSpec(memory_space=pltpu.SMEM)
PARAMS = pltpu.CompilerParams(vmem_limit_bytes=40 * 1024 * 1024)


def pick_kernel(picks_hbm, counts_hbm, points_hbm, out_ref, picks_ref, counts_ref, points_ref, sems):
    copies = [
        pltpu.make_async_copy(picks_hbm, picks_ref, sems.at[0]),
        pltpu.make_async_copy(counts_hbm, counts_ref, sems.at[1]),
        pltpu.make_async_copy(points_hbm, points_ref, sems.at[2]),
    ]
    for copy in copies:
        copy.start()
    rounds, most = picks_ref.shape
    rows = points_ref.shape[0]
    slot = lax.broadcasted_iota(jnp.int32, (1, most), 1)
    diagonal = lax.broadcasted_iota(jnp.int32, (most, most), 0) == lax.broadcasted_iota(
        jnp.int32, (most, most), 1
    )
    column = lax.broadcasted_iota(jnp.int32, (most, rows), 1)
    copies[0].wait()
    copies[1].wait()
    select = []
    for step in range(rounds):
        picked = picks_ref[step : step + 1, :]
        named = jnp.where(slot < counts_ref[step], picked, picked[:, :1])
        down = jnp.sum(jnp.where(diagonal, named, 0), axis=1, keepdims=True)
        select.append(jnp.where(column == down, 1.0, 0.0).astype(BF16))
    select = jnp.concatenate(select, axis=0)
    copies[2].wait()
    cand = jnp.dot(select, points_ref[...], preferred_element_type=F32).astype(BF16)
    for place in range(out_ref.shape[0]):
        out_ref[place] = cand


def pick_rows(picks, counts, points, copies):
    slots = picks.shape[0] * picks.shape[1]
    rows, width = points.shape
    return pl.pallas_call(
        pick_kernel,
        out_shape=jax.ShapeDtypeStruct((copies, slots, width), BF16),
        in_specs=[ANY, ANY, ANY],
        out_specs=VMEM,
        scratch_shapes=[
            pltpu.VMEM(picks.shape, jnp.int32),
            pltpu.SMEM(counts.shape, jnp.int32),
            pltpu.VMEM(points.shape, BF16),
            pltpu.SemaphoreType.DMA((3,)),
        ],
        compiler_params=pltpu.CompilerParams(vmem_limit_bytes=60 * 1024 * 1024),
        cost_estimate=pl.CostEstimate(
            flops=2 * slots * rows * width, bytes_accessed=rows * width * 2, transcendentals=0
        ),
    )(picks, counts, points)


def turn_kernel(*refs):
    blocks, (turned_ref, length_ref) = refs[:-2], refs[-2:]
    width = turned_ref.shape[1]
    place = 0
    for block_ref in blocks:
        rows = block_ref.shape[0]
        number, start = divmod(place, turned_ref.shape[2])
        turned = (block_ref[...] * BF16(-2.0)).T
        turned_ref[number, :, start : start + rows] = turned
        wide = turned.astype(F32)
        length_ref[number, :, start : start + rows] = jnp.sum(wide * wide, axis=0, keepdims=True) * 0.25
        place += rows


def turn(blocks, rows):
    width = blocks[0].shape[1]
    count = sum(block.shape[0] for block in blocks) // rows
    return pl.pallas_call(
        turn_kernel,
        out_shape=(
            jax.ShapeDtypeStruct((count, width, rows), BF16),
            jax.ShapeDtypeStruct((count, 1, rows), F32),
        ),
        in_specs=[VMEM] * len(blocks),
        out_specs=(VMEM, VMEM),
        compiler_params=PARAMS,
        cost_estimate=pl.CostEstimate(
            flops=count * rows * width * 3, bytes_accessed=count * rows * width * 4, transcendentals=0
        ),
    )(*blocks)


def half_round(cand_ref, step, rounds):
    sources, slots, width = cand_ref.shape
    most = slots // rounds
    return cand_ref[:, step * most : (step + 1) * most, :].reshape(sources * most, width)


def squares_of(cands, sq_ref, rounds):
    for step in range(rounds):
        base = 0
        for cand_ref in cands:
            values = half_round(cand_ref, step, rounds).astype(F32)
            squares = jnp.sum(values * values, axis=1, keepdims=True)
            rows = values.shape[0]
            sq_ref[step, base : base + rows] = jnp.broadcast_to(squares, (rows, LANES))
            base += rows


def lowest(weights, cands, sq_ref, step, rounds, skipped=0):
    count = weights.shape[1]
    best = None
    base = 0
    for order, cand_ref in enumerate(cands):
        values = half_round(cand_ref, step, rounds)
        if order < skipped:
            base += values.shape[0]
            continue
        for part in range(0, values.shape[0], PART):
            piece = values[part : part + PART]
            size = piece.shape[0]
            inner = jnp.dot(piece, weights, preferred_element_type=F32)
            squares = sq_ref[step, base : base + size, :]
            dist = inner + jnp.concatenate([squares] * (count // LANES), axis=1)
            low = jnp.min(dist.reshape(size // 8, 8, count), axis=0)
            best = low if best is None else jnp.minimum(best, low)
            base += size
    return jnp.min(best, axis=0, keepdims=True)


def blocks_of(turned):
    return [(ref, number) for ref in turned for number in range(ref.shape[0])]


def near_cost(turned, cands):
    columns = sum(block.shape[0] * block.shape[2] for block in turned)
    return pl.CostEstimate(
        flops=2 * columns * sum(cand.size for cand in cands),
        bytes_accessed=2 * sum(x.size for x in turned + cands),
        transcendentals=0,
    )


def near(turned, cands, low, rounds, done=0):
    count, rows = sum(block.shape[0] for block in turned), turned[0].shape[2]

    def body(*refs):
        turned_refs, refs = refs[: len(turned)], refs[len(turned) :]
        cand_refs, refs = refs[: len(cands)], refs[len(cands) :]
        out_ref, sq_ref = refs[-2:]
        squares_of(cand_refs, sq_ref, rounds)
        for place, (ref, number) in enumerate(blocks_of(turned_refs)):
            known = low is not None and place < low.shape[0]
            skipped = done if known else 0
            for step in range(rounds):
                value = lowest(ref[number], cand_refs, sq_ref, step, rounds, skipped)
                if known:
                    value = jnp.minimum(value, refs[0][place, step : step + 1, :])
                out_ref[place, step : step + 1, :] = value

    extra = [] if low is None else [low]
    slots = sum(cand.shape[0] * cand.shape[1] for cand in cands)
    return pl.pallas_call(
        body,
        out_shape=jax.ShapeDtypeStruct((count, rounds, rows), F32),
        in_specs=[VMEM] * (len(turned) + len(cands) + len(extra)),
        out_specs=VMEM,
        scratch_shapes=[pltpu.VMEM((rounds, slots // rounds, LANES), F32)],
        compiler_params=PARAMS,
        cost_estimate=near_cost(turned, cands),
    )(*turned, *cands, *extra)


def last_near(turned, cands, low, lengths, init_row, rounds):
    count, rows = sum(block.shape[0] for block in turned), turned[0].shape[2]

    def body(*refs):
        turned_refs, refs = refs[: len(turned)], refs[len(turned) :]
        length_refs, refs = refs[: len(turned)], refs[len(turned) :]
        cand_refs, refs = refs[: len(cands)], refs[len(cands) :]
        low_ref, init_ref, out_ref, sq_ref = refs
        squares_of(cand_refs, sq_ref, rounds)
        blocks = zip(blocks_of(turned_refs), blocks_of(length_refs))
        for number, ((ref, inner), (length_ref, _)) in enumerate(blocks):
            for step in range(rounds):
                value = lowest(ref[inner], cand_refs, sq_ref, step, rounds)
                value = jnp.minimum(value, low_ref[number, step : step + 1, :])
                dist = jnp.maximum(value + length_ref[inner], 0.0)
                if number == 0:
                    dist = jnp.minimum(dist, init_ref[...])
                out_ref[step, number : number + 1, :] = dist

    slots = sum(cand.shape[0] * cand.shape[1] for cand in cands)
    return pl.pallas_call(
        body,
        out_shape=jax.ShapeDtypeStruct((rounds, count, rows), F32),
        in_specs=[VMEM] * (len(turned) + len(lengths) + len(cands) + 2),
        out_specs=VMEM,
        scratch_shapes=[pltpu.VMEM((rounds, slots // rounds, LANES), F32)],
        compiler_params=PARAMS,
        cost_estimate=near_cost(turned, cands),
    )(*turned, *lengths, *cands, low, init_row)


def totals(dists, shifts, peers):
    rounds, count, rows = dists[0].shape

    def body(*refs):
        dist_refs, (own_ref, total_ref) = refs[: len(dists)], refs[len(dists) :]
        lane = lax.broadcasted_iota(jnp.int32, total_ref.shape, 1)
        total = jnp.zeros(total_ref.shape, F32)
        current = [None] * count
        for step in range(rounds):
            for number in range(count):
                for ref, by in zip(dist_refs, (0, *shifts)):
                    there = PLACES.index((PLACES[number] + by) % count)
                    dist = ref[step, there : there + 1, :]
                    best = current[number]
                    current[number] = dist if best is None else jnp.minimum(best, dist)
            cost = jnp.sum(sum(current), axis=1, keepdims=True)
            total = jnp.where(lane == step, cost, total)
        total_ref[...] = total
        own_ref[...] = current[0]

    return pl.pallas_call(
        body,
        out_shape=(
            jax.ShapeDtypeStruct((1, rows), F32),
            jax.ShapeDtypeStruct((peers, LANES), F32),
        ),
        in_specs=[VMEM] * len(dists),
        out_specs=(VMEM, VMEM),
        compiler_params=PARAMS,
    )(*dists)


def finish(own, shares, rounds, all_rows):
    def body(own_ref, share_ref, min_ref, normal_ref, cost_ref):
        total = jnp.sum(share_ref[...], axis=0, keepdims=True)
        cost_ref[...] = total[:, :rounds]
        min_ref[...] = own_ref[...]
        normal_ref[...] = own_ref[...] * all_rows / total[:, rounds - 1 : rounds]

    row = jax.ShapeDtypeStruct(own.shape, F32)
    return pl.pallas_call(
        body,
        out_shape=(row, row, jax.ShapeDtypeStruct((1, rounds), F32)),
        in_specs=[VMEM, VMEM],
        out_specs=(VMEM, VMEM, VMEM),
        compiler_params=PARAMS,
    )(own, shares)


def shift(block, axis, size, by):
    return lax.ppermute(block, axis, [(i, (i + by) % size) for i in range(size)])


def shards(points, init_dist, picks, pick_counts):
    rounds, most = picks.shape
    rows, width = points.shape
    subs = lax.axis_size("y")
    half = rows // 2
    behind, ahead = (shift(points, "y", subs, by) for by in (1, 3))
    across = [shift(behind[:half], "y", subs, 1), shift(ahead[half:], "y", subs, 3)]
    cand = pick_rows(picks, pick_counts.reshape(-1), points, CHIPS_Z)
    along_z = lax.all_to_all(cand, "z", 0, 0, tiled=True)
    from_x = [shift(along_z, "x", CHIPS_X, by) for by in (2, 1, 3)]
    opposite, after, before = from_x
    swapped = shift(along_z, "c", CORES, 1)
    near_turned, near_lengths = turn([points, behind, ahead], rows)
    far_turned, far_lengths = turn(across, rows)
    turned, lengths = [near_turned, far_turned], [near_lengths, far_lengths]
    low = near([near_turned], [along_z], None, rounds)
    low = near(turned, [along_z, swapped], low, rounds, 1)
    beside = [shift(piece, "c", CORES, 1) for piece in (after, before)]
    low = near(turned, [after, before], low, rounds)
    low = near(turned, beside, low, rounds)
    opposite, low = lax.optimization_barrier((opposite, low))
    last = shift(opposite, "c", CORES, 1)
    low = near(turned, [opposite], low, rounds)
    last = [last]
    dist = last_near(turned, last, low, lengths, init_dist[None], rounds)
    shared = [dist] + [shift(dist, "y", subs, by) for by in (2, 1, 3)]
    own, total = totals(shared, (2, 1, 3), lax.axis_size(("z", "x")))
    total = total + shift(total, "c", CORES, 1)
    shares = lax.all_to_all(total, ("z", "x"), 0, 0, tiled=True)
    all_rows = float(rows * lax.axis_size(("z", "x", "c", "y")))
    min_dist, normalized, round_costs = finish(own, shares, rounds, all_rows)
    return (min_dist[0], normalized[0], round_costs[0])


def solution(mesh):
    fine = Mesh(
        mesh.devices.reshape(CHIPS_Z, CHIPS_X, CORES, mesh.shape["sub"]), ("z", "x", "c", "y")
    )
    rows = ("z", "x", "c", "y")
    return jax.shard_map(
        shards,
        mesh=fine,
        in_specs=(P(rows, None), P(rows), P(None, rows), P(None, rows)),
        out_specs=(P(rows), P(rows), P()),
        check_vma=False,
    )
```

```python
import jax
import jax.numpy as jnp
from jax import lax
from jax.experimental import pallas as pl
from jax.experimental.pallas import tpu as pltpu
from jax.sharding import Mesh, PartitionSpec as P

CHIPS_Z, CHIPS_X, CORES = 8, 4, 2
PART = 256
LANES = 128
PLACES = (0, 3, 1, 2)
F32, BF16 = jnp.float32, jnp.bfloat16
VMEM = pl.BlockSpec(memory_space=pltpu.VMEM)
ANY = pl.BlockSpec(memory_space=pl.ANY)
SMEM = pl.BlockSpec(memory_space=pltpu.SMEM)
PARAMS = pltpu.CompilerParams(vmem_limit_bytes=40 * 1024 * 1024)


def pick_kernel(picks_hbm, counts_hbm, points_hbm, out_ref, picks_ref, counts_ref, points_ref, sems):
    copies = [
        pltpu.make_async_copy(picks_hbm, picks_ref, sems.at[0]),
        pltpu.make_async_copy(counts_hbm, counts_ref, sems.at[1]),
        pltpu.make_async_copy(points_hbm, points_ref, sems.at[2]),
    ]
    for copy in copies:
        copy.start()
    rounds, most = picks_ref.shape
    rows = points_ref.shape[0]
    slot = lax.broadcasted_iota(jnp.int32, (1, most), 1)
    diagonal = lax.broadcasted_iota(jnp.int32, (most, most), 0) == lax.broadcasted_iota(
        jnp.int32, (most, most), 1
    )
    column = lax.broadcasted_iota(jnp.int32, (most, rows), 1)
    copies[0].wait()
    copies[1].wait()
    select = []
    for step in range(rounds):
        picked = picks_ref[step : step + 1, :]
        named = jnp.where(slot < counts_ref[step], picked, picked[:, :1])
        down = jnp.sum(jnp.where(diagonal, named, 0), axis=1, keepdims=True)
        select.append(jnp.where(column == down, 1.0, 0.0).astype(BF16))
    select = jnp.concatenate(select, axis=0)
    copies[2].wait()
    cand = jnp.dot(select, points_ref[...], preferred_element_type=F32).astype(BF16)
    for place in range(out_ref.shape[0]):
        out_ref[place] = cand


def pick_rows(picks, counts, points, copies):
    slots = picks.shape[0] * picks.shape[1]
    rows, width = points.shape
    return pl.pallas_call(
        pick_kernel,
        out_shape=jax.ShapeDtypeStruct((copies, slots, width), BF16),
        in_specs=[ANY, ANY, ANY],
        out_specs=VMEM,
        scratch_shapes=[
            pltpu.VMEM(picks.shape, jnp.int32),
            pltpu.SMEM(counts.shape, jnp.int32),
            pltpu.VMEM(points.shape, BF16),
            pltpu.SemaphoreType.DMA((3,)),
        ],
        compiler_params=pltpu.CompilerParams(vmem_limit_bytes=60 * 1024 * 1024),
        cost_estimate=pl.CostEstimate(
            flops=2 * slots * rows * width, bytes_accessed=rows * width * 2, transcendentals=0
        ),
    )(picks, counts, points)


def turn_kernel(*refs):
    blocks, (turned_ref, length_ref) = refs[:-2], refs[-2:]
    width = turned_ref.shape[1]
    place = 0
    for block_ref in blocks:
        rows = block_ref.shape[0]
        number, start = divmod(place, turned_ref.shape[2])
        turned = (block_ref[...] * BF16(-2.0)).T
        turned_ref[number, :, start : start + rows] = turned
        wide = turned.astype(F32)
        length_ref[number, :, start : start + rows] = jnp.sum(wide * wide, axis=0, keepdims=True) * 0.25
        place += rows


def turn(blocks, rows):
    width = blocks[0].shape[1]
    count = sum(block.shape[0] for block in blocks) // rows
    return pl.pallas_call(
        turn_kernel,
        out_shape=(
            jax.ShapeDtypeStruct((count, width, rows), BF16),
            jax.ShapeDtypeStruct((count, 1, rows), F32),
        ),
        in_specs=[VMEM] * len(blocks),
        out_specs=(VMEM, VMEM),
        compiler_params=PARAMS,
        cost_estimate=pl.CostEstimate(
            flops=count * rows * width * 3, bytes_accessed=count * rows * width * 4, transcendentals=0
        ),
    )(*blocks)


def half_round(cand_ref, step, rounds):
    sources, slots, width = cand_ref.shape
    most = slots // rounds
    return cand_ref[:, step * most : (step + 1) * most, :].reshape(sources * most, width)


def squares_of(cands, sq_ref, rounds):
    for step in range(rounds):
        base = 0
        for cand_ref in cands:
            values = half_round(cand_ref, step, rounds).astype(F32)
            squares = jnp.sum(values * values, axis=1, keepdims=True)
            rows = values.shape[0]
            sq_ref[step, base : base + rows] = jnp.broadcast_to(squares, (rows, LANES))
            base += rows


def lowest(weights, cands, sq_ref, step, rounds, skipped=0):
    count = weights.shape[1]
    best = None
    base = 0
    for order, cand_ref in enumerate(cands):
        values = half_round(cand_ref, step, rounds)
        if order < skipped:
            base += values.shape[0]
            continue
        for part in range(0, values.shape[0], PART):
            piece = values[part : part + PART]
            size = piece.shape[0]
            inner = jnp.dot(piece, weights, preferred_element_type=F32)
            squares = sq_ref[step, base : base + size, :]
            dist = inner + jnp.concatenate([squares] * (count // LANES), axis=1)
            low = jnp.min(dist.reshape(size // 8, 8, count), axis=0)
            best = low if best is None else jnp.minimum(best, low)
            base += size
    return jnp.min(best, axis=0, keepdims=True)


def blocks_of(turned):
    return [(ref, number) for ref in turned for number in range(ref.shape[0])]


def near_cost(turned, cands):
    columns = sum(block.shape[0] * block.shape[2] for block in turned)
    return pl.CostEstimate(
        flops=2 * columns * sum(cand.size for cand in cands),
        bytes_accessed=2 * sum(x.size for x in turned + cands),
        transcendentals=0,
    )


def near(turned, cands, low, rounds, done=0):
    count, rows = sum(block.shape[0] for block in turned), turned[0].shape[2]

    def body(*refs):
        turned_refs, refs = refs[: len(turned)], refs[len(turned) :]
        cand_refs, refs = refs[: len(cands)], refs[len(cands) :]
        out_ref, sq_ref = refs[-2:]
        squares_of(cand_refs, sq_ref, rounds)
        for place, (ref, number) in enumerate(blocks_of(turned_refs)):
            known = low is not None and place < low.shape[0]
            skipped = done if known else 0
            for step in range(rounds):
                value = lowest(ref[number], cand_refs, sq_ref, step, rounds, skipped)
                if known:
                    value = jnp.minimum(value, refs[0][place, step : step + 1, :])
                out_ref[place, step : step + 1, :] = value

    extra = [] if low is None else [low]
    slots = sum(cand.shape[0] * cand.shape[1] for cand in cands)
    return pl.pallas_call(
        body,
        out_shape=jax.ShapeDtypeStruct((count, rounds, rows), F32),
        in_specs=[VMEM] * (len(turned) + len(cands) + len(extra)),
        out_specs=VMEM,
        scratch_shapes=[pltpu.VMEM((rounds, slots // rounds, LANES), F32)],
        compiler_params=PARAMS,
        cost_estimate=near_cost(turned, cands),
    )(*turned, *cands, *extra)


def last_near(turned, cands, low, lengths, init_row, rounds):
    count, rows = sum(block.shape[0] for block in turned), turned[0].shape[2]

    def body(*refs):
        turned_refs, refs = refs[: len(turned)], refs[len(turned) :]
        length_refs, refs = refs[: len(turned)], refs[len(turned) :]
        cand_refs, refs = refs[: len(cands)], refs[len(cands) :]
        low_ref, init_ref, out_ref, sq_ref = refs
        squares_of(cand_refs, sq_ref, rounds)
        blocks = zip(blocks_of(turned_refs), blocks_of(length_refs))
        for number, ((ref, inner), (length_ref, _)) in enumerate(blocks):
            for step in range(rounds):
                value = lowest(ref[inner], cand_refs, sq_ref, step, rounds)
                value = jnp.minimum(value, low_ref[number, step : step + 1, :])
                dist = jnp.maximum(value + length_ref[inner], 0.0)
                if number == 0:
                    dist = jnp.minimum(dist, init_ref[...])
                out_ref[step, number : number + 1, :] = dist

    slots = sum(cand.shape[0] * cand.shape[1] for cand in cands)
    return pl.pallas_call(
        body,
        out_shape=jax.ShapeDtypeStruct((rounds, count, rows), F32),
        in_specs=[VMEM] * (len(turned) + len(lengths) + len(cands) + 2),
        out_specs=VMEM,
        scratch_shapes=[pltpu.VMEM((rounds, slots // rounds, LANES), F32)],
        compiler_params=PARAMS,
        cost_estimate=near_cost(turned, cands),
    )(*turned, *lengths, *cands, low, init_row)


def totals(dists, shifts, peers):
    rounds, count, rows = dists[0].shape

    def body(*refs):
        dist_refs, (own_ref, total_ref) = refs[: len(dists)], refs[len(dists) :]
        lane = lax.broadcasted_iota(jnp.int32, total_ref.shape, 1)
        total = jnp.zeros(total_ref.shape, F32)
        current = [None] * count
        for step in range(rounds):
            for number in range(count):
                for ref, by in zip(dist_refs, (0, *shifts)):
                    there = PLACES.index((PLACES[number] + by) % count)
                    dist = ref[step, there : there + 1, :]
                    best = current[number]
                    current[number] = dist if best is None else jnp.minimum(best, dist)
            pairs = (current[0] + current[3]) + (current[1] + current[2])
            cost = jnp.sum(pairs, axis=1, keepdims=True)
            total = jnp.where(lane == step, cost, total)
        total_ref[...] = total
        own_ref[...] = current[0]

    return pl.pallas_call(
        body,
        out_shape=(
            jax.ShapeDtypeStruct((1, rows), F32),
            jax.ShapeDtypeStruct((peers, LANES), F32),
        ),
        in_specs=[VMEM] * len(dists),
        out_specs=(VMEM, VMEM),
        compiler_params=PARAMS,
    )(*dists)


def finish(own, shares, rounds, all_rows):
    def body(own_ref, share_ref, min_ref, normal_ref, cost_ref):
        total = jnp.sum(share_ref[...], axis=0, keepdims=True)
        cost_ref[...] = total[:, :rounds]
        min_ref[...] = own_ref[...]
        normal_ref[...] = own_ref[...] * all_rows / total[:, rounds - 1 : rounds]

    row = jax.ShapeDtypeStruct(own.shape, F32)
    return pl.pallas_call(
        body,
        out_shape=(row, row, jax.ShapeDtypeStruct((1, rounds), F32)),
        in_specs=[VMEM, VMEM],
        out_specs=(VMEM, VMEM, VMEM),
        compiler_params=PARAMS,
    )(own, shares)


def shift(block, axis, size, by):
    return lax.ppermute(block, axis, [(i, (i + by) % size) for i in range(size)])


def shards(points, init_dist, picks, pick_counts):
    rounds, most = picks.shape
    rows, width = points.shape
    subs = lax.axis_size("y")
    half = rows // 2
    behind, ahead = (shift(points, "y", subs, by) for by in (1, 3))
    across = [shift(behind[:half], "y", subs, 1), shift(ahead[half:], "y", subs, 3)]
    cand = pick_rows(picks, pick_counts.reshape(-1), points, CHIPS_Z)
    along_z = lax.all_to_all(cand, "z", 0, 0, tiled=True)
    from_x = [shift(along_z, "x", CHIPS_X, by) for by in (2, 1, 3)]
    opposite, after, before = from_x
    near_turned, near_lengths = turn([points, behind, ahead], rows)
    far_turned, far_lengths = turn(across, rows)
    turned, lengths = [near_turned, far_turned], [near_lengths, far_lengths]
    low = near([near_turned], [along_z], None, rounds)
    also = along_z
    beside = [shift(piece, "c", CORES, 1) for piece in (also, after, before)]
    low = near(turned, [along_z, after, before], low, rounds, 1)
    low = near(turned, beside, low, rounds)
    opposite, low = lax.optimization_barrier((opposite, low))
    last = [shift(opposite, "c", CORES, 1)]
    low = near(turned, [opposite], low, rounds)
    dist = last_near(turned, last, low, lengths, init_dist[None], rounds)
    shared = [dist] + [shift(dist, "y", subs, by) for by in (2, 1, 3)]
    own, total = totals(shared, (2, 1, 3), lax.axis_size(("z", "x")))
    total = total + shift(total, "c", CORES, 1)
    shares = lax.all_to_all(total, ("z", "x"), 0, 0, tiled=True)
    all_rows = float(rows * lax.axis_size(("z", "x", "c", "y")))
    min_dist, normalized, round_costs = finish(own, shares, rounds, all_rows)
    return (min_dist[0], normalized[0], round_costs[0])


def solution(mesh):
    fine = Mesh(
        mesh.devices.reshape(CHIPS_Z, CHIPS_X, CORES, mesh.shape["sub"]), ("z", "x", "c", "y")
    )
    rows = ("z", "x", "c", "y")
    return jax.shard_map(
        shards,
        mesh=fine,
        in_specs=(P(rows, None), P(rows), P(None, rows), P(None, rows)),
        out_specs=(P(rows), P(rows), P()),
        check_vma=False,
    )
```

```python
import jax
import jax.numpy as jnp
from jax import lax
from jax.experimental import pallas as pl
from jax.experimental.pallas import tpu as pltpu
from jax.sharding import Mesh, PartitionSpec as P

CHIPS_Z, CHIPS_X, CORES = 8, 4, 2
PART = 256
LANES = 128
COLUMNS = 512
PLACES = (0, 3, 1, 2)
F32, BF16 = jnp.float32, jnp.bfloat16
VMEM = pl.BlockSpec(memory_space=pltpu.VMEM)
ANY = pl.BlockSpec(memory_space=pl.ANY)
SMEM = pl.BlockSpec(memory_space=pltpu.SMEM)
PARAMS = pltpu.CompilerParams(vmem_limit_bytes=40 * 1024 * 1024)


def pick_kernel(picks_hbm, counts_hbm, points_hbm, out_ref, picks_ref, counts_ref, points_ref, sems):
    copies = [
        pltpu.make_async_copy(picks_hbm, picks_ref, sems.at[0]),
        pltpu.make_async_copy(counts_hbm, counts_ref, sems.at[1]),
        pltpu.make_async_copy(points_hbm, points_ref, sems.at[2]),
    ]
    for copy in copies:
        copy.start()
    rounds, most = picks_ref.shape
    rows = points_ref.shape[0]
    slot = lax.broadcasted_iota(jnp.int32, (1, most), 1)
    diagonal = lax.broadcasted_iota(jnp.int32, (most, most), 0) == lax.broadcasted_iota(
        jnp.int32, (most, most), 1
    )
    column = lax.broadcasted_iota(jnp.int32, (most, rows), 1)
    copies[0].wait()
    copies[1].wait()
    select = []
    for step in range(rounds):
        picked = picks_ref[step : step + 1, :]
        named = jnp.where(slot < counts_ref[step], picked, picked[:, :1])
        down = jnp.sum(jnp.where(diagonal, named, 0), axis=1, keepdims=True)
        select.append(jnp.where(column == down, 1.0, 0.0).astype(BF16))
    select = jnp.concatenate(select, axis=0)
    copies[2].wait()
    cand = jnp.dot(select, points_ref[...], preferred_element_type=F32).astype(BF16)
    for place in range(out_ref.shape[0]):
        out_ref[place] = cand


def pick_rows(picks, counts, points, copies):
    slots = picks.shape[0] * picks.shape[1]
    rows, width = points.shape
    return pl.pallas_call(
        pick_kernel,
        out_shape=jax.ShapeDtypeStruct((copies, slots, width), BF16),
        in_specs=[ANY, ANY, ANY],
        out_specs=VMEM,
        scratch_shapes=[
            pltpu.VMEM(picks.shape, jnp.int32),
            pltpu.SMEM(counts.shape, jnp.int32),
            pltpu.VMEM(points.shape, BF16),
            pltpu.SemaphoreType.DMA((3,)),
        ],
        compiler_params=pltpu.CompilerParams(vmem_limit_bytes=60 * 1024 * 1024),
        cost_estimate=pl.CostEstimate(
            flops=2 * slots * rows * width, bytes_accessed=rows * width * 2, transcendentals=0
        ),
    )(picks, counts, points)


def turn_kernel(*refs):
    blocks, (turned_ref, length_ref) = refs[:-2], refs[-2:]
    width = turned_ref.shape[1]
    place = 0
    for block_ref in blocks:
        rows = block_ref.shape[0]
        number, start = divmod(place, turned_ref.shape[2])
        turned = (block_ref[...] * BF16(-2.0)).T
        turned_ref[number, :, start : start + rows] = turned
        wide = turned.astype(F32)
        length_ref[number, :, start : start + rows] = jnp.sum(wide * wide, axis=0, keepdims=True) * 0.25
        place += rows


def turn(blocks, rows):
    width = blocks[0].shape[1]
    count = sum(block.shape[0] for block in blocks) // rows
    return pl.pallas_call(
        turn_kernel,
        out_shape=(
            jax.ShapeDtypeStruct((count, width, rows), BF16),
            jax.ShapeDtypeStruct((count, 1, rows), F32),
        ),
        in_specs=[VMEM] * len(blocks),
        out_specs=(VMEM, VMEM),
        compiler_params=PARAMS,
        cost_estimate=pl.CostEstimate(
            flops=count * rows * width * 3, bytes_accessed=count * rows * width * 4, transcendentals=0
        ),
    )(*blocks)


def half_round(cand_ref, step, rounds):
    sources, slots, width = cand_ref.shape
    most = slots // rounds
    return cand_ref[:, step * most : (step + 1) * most, :].reshape(sources * most, width)


def squares_of(cands, sq_ref, rounds):
    for step in range(rounds):
        base = 0
        for cand_ref in cands:
            values = half_round(cand_ref, step, rounds).astype(F32)
            squares = jnp.sum(values * values, axis=1, keepdims=True)
            rows = values.shape[0]
            sq_ref[step, base : base + rows] = jnp.broadcast_to(squares, (rows, LANES))
            base += rows


def lowest(weights, cands, sq_ref, step, rounds, skipped=0):
    found = []
    for column in range(0, weights.shape[1], COLUMNS):
        tile = weights[:, column : column + COLUMNS]
        best = None
        base = 0
        for order, cand_ref in enumerate(cands):
            values = half_round(cand_ref, step, rounds)
            if order < skipped:
                base += values.shape[0]
                continue
            for part in range(0, values.shape[0], PART):
                piece = values[part : part + PART]
                size = piece.shape[0]
                inner = jnp.dot(piece, tile, preferred_element_type=F32)
                squares = sq_ref[step, base : base + size, :]
                dist = inner + jnp.concatenate([squares] * (COLUMNS // LANES), axis=1)
                low = jnp.min(dist.reshape(size // 8, 8, COLUMNS), axis=0)
                best = low if best is None else jnp.minimum(best, low)
                base += size
        found.append(jnp.min(best, axis=0, keepdims=True))
    return jnp.concatenate(found, axis=1)


def blocks_of(turned):
    return [(ref, number) for ref in turned for number in range(ref.shape[0])]


def near_cost(turned, cands):
    columns = sum(block.shape[0] * block.shape[2] for block in turned)
    return pl.CostEstimate(
        flops=2 * columns * sum(cand.size for cand in cands),
        bytes_accessed=2 * sum(x.size for x in turned + cands),
        transcendentals=0,
    )


def near(turned, cands, low, rounds, done=0):
    count, rows = sum(block.shape[0] for block in turned), turned[0].shape[2]

    def body(*refs):
        turned_refs, refs = refs[: len(turned)], refs[len(turned) :]
        cand_refs, refs = refs[: len(cands)], refs[len(cands) :]
        out_ref, sq_ref = refs[-2:]
        squares_of(cand_refs, sq_ref, rounds)
        for place, (ref, number) in enumerate(blocks_of(turned_refs)):
            known = low is not None and place < low.shape[0]
            skipped = done if known else 0
            for step in range(rounds):
                value = lowest(ref[number], cand_refs, sq_ref, step, rounds, skipped)
                if known:
                    value = jnp.minimum(value, refs[0][place, step : step + 1, :])
                out_ref[place, step : step + 1, :] = value

    extra = [] if low is None else [low]
    slots = sum(cand.shape[0] * cand.shape[1] for cand in cands)
    return pl.pallas_call(
        body,
        out_shape=jax.ShapeDtypeStruct((count, rounds, rows), F32),
        in_specs=[VMEM] * (len(turned) + len(cands) + len(extra)),
        out_specs=VMEM,
        scratch_shapes=[pltpu.VMEM((rounds, slots // rounds, LANES), F32)],
        compiler_params=PARAMS,
        cost_estimate=near_cost(turned, cands),
    )(*turned, *cands, *extra)


def last_near(turned, cands, low, lengths, init_row, rounds):
    count, rows = sum(block.shape[0] for block in turned), turned[0].shape[2]

    def body(*refs):
        turned_refs, refs = refs[: len(turned)], refs[len(turned) :]
        length_refs, refs = refs[: len(turned)], refs[len(turned) :]
        cand_refs, refs = refs[: len(cands)], refs[len(cands) :]
        low_ref, init_ref, out_ref, sq_ref = refs
        squares_of(cand_refs, sq_ref, rounds)
        blocks = zip(blocks_of(turned_refs), blocks_of(length_refs))
        for number, ((ref, inner), (length_ref, _)) in enumerate(blocks):
            for step in range(rounds):
                value = lowest(ref[inner], cand_refs, sq_ref, step, rounds)
                value = jnp.minimum(value, low_ref[number, step : step + 1, :])
                dist = jnp.maximum(value + length_ref[inner], 0.0)
                if number == 0:
                    dist = jnp.minimum(dist, init_ref[...])
                out_ref[step, number : number + 1, :] = dist

    slots = sum(cand.shape[0] * cand.shape[1] for cand in cands)
    return pl.pallas_call(
        body,
        out_shape=jax.ShapeDtypeStruct((rounds, count, rows), F32),
        in_specs=[VMEM] * (len(turned) + len(lengths) + len(cands) + 2),
        out_specs=VMEM,
        scratch_shapes=[pltpu.VMEM((rounds, slots // rounds, LANES), F32)],
        compiler_params=PARAMS,
        cost_estimate=near_cost(turned, cands),
    )(*turned, *lengths, *cands, low, init_row)


def totals(dists, shifts, peers):
    rounds, count, rows = dists[0].shape

    def body(*refs):
        dist_refs, (own_ref, total_ref) = refs[: len(dists)], refs[len(dists) :]
        lane = lax.broadcasted_iota(jnp.int32, total_ref.shape, 1)
        total = jnp.zeros(total_ref.shape, F32)
        current = [None] * count
        for step in range(rounds):
            for number in range(count):
                for ref, by in zip(dist_refs, (0, *shifts)):
                    there = PLACES.index((PLACES[number] + by) % count)
                    dist = ref[step, there : there + 1, :]
                    best = current[number]
                    current[number] = dist if best is None else jnp.minimum(best, dist)
            pairs = (current[0] + current[3]) + (current[1] + current[2])
            cost = jnp.sum(pairs, axis=1, keepdims=True)
            total = jnp.where(lane == step, cost, total)
        total_ref[...] = total
        own_ref[...] = current[0]

    return pl.pallas_call(
        body,
        out_shape=(
            jax.ShapeDtypeStruct((1, rows), F32),
            jax.ShapeDtypeStruct((peers, LANES), F32),
        ),
        in_specs=[VMEM] * len(dists),
        out_specs=(VMEM, VMEM),
        compiler_params=PARAMS,
    )(*dists)


def finish(own, shares, rounds, all_rows):
    def body(own_ref, share_ref, min_ref, normal_ref, cost_ref):
        total = jnp.sum(share_ref[...], axis=0, keepdims=True)
        cost_ref[...] = total[:, :rounds]
        min_ref[...] = own_ref[...]
        normal_ref[...] = own_ref[...] * all_rows / total[:, rounds - 1 : rounds]

    row = jax.ShapeDtypeStruct(own.shape, F32)
    return pl.pallas_call(
        body,
        out_shape=(row, row, jax.ShapeDtypeStruct((1, rounds), F32)),
        in_specs=[VMEM, VMEM],
        out_specs=(VMEM, VMEM, VMEM),
        compiler_params=PARAMS,
    )(own, shares)


def shift(block, axis, size, by):
    return lax.ppermute(block, axis, [(i, (i + by) % size) for i in range(size)])


def shards(points, init_dist, picks, pick_counts):
    rounds, most = picks.shape
    rows, width = points.shape
    subs = lax.axis_size("y")
    half = rows // 2
    behind, ahead = (shift(points, "y", subs, by) for by in (1, 3))
    across = [shift(behind[:half], "y", subs, 1), shift(ahead[half:], "y", subs, 3)]
    cand = pick_rows(picks, pick_counts.reshape(-1), points, CHIPS_Z)
    along_z = lax.all_to_all(cand, "z", 0, 0, tiled=True)
    from_x = [shift(along_z, "x", CHIPS_X, by) for by in (2, 1, 3)]
    opposite, after, before = from_x
    near_turned, near_lengths = turn([points, behind, ahead], rows)
    far_turned, far_lengths = turn(across, rows)
    turned, lengths = [near_turned, far_turned], [near_lengths, far_lengths]
    low = near([near_turned], [along_z], None, rounds)
    also = along_z
    beside = [shift(piece, "c", CORES, 1) for piece in (after, before, also)]
    low = near(turned, [along_z, after, before], low, rounds, 1)
    low = near(turned, beside, low, rounds)
    opposite, low = lax.optimization_barrier((opposite, low))
    last = [shift(opposite, "c", CORES, 1)]
    low = near(turned, [opposite], low, rounds)
    dist = last_near(turned, last, low, lengths, init_dist[None], rounds)
    shared = [dist] + [shift(dist, "y", subs, by) for by in (2, 1, 3)]
    own, total = totals(shared, (2, 1, 3), lax.axis_size(("z", "x")))
    total = total + shift(total, "c", CORES, 1)
    shares = lax.all_to_all(total, ("z", "x"), 0, 0, tiled=True)
    all_rows = float(rows * lax.axis_size(("z", "x", "c", "y")))
    min_dist, normalized, round_costs = finish(own, shares, rounds, all_rows)
    return (min_dist[0], normalized[0], round_costs[0])


def solution(mesh):
    fine = Mesh(
        mesh.devices.reshape(CHIPS_Z, CHIPS_X, CORES, mesh.shape["sub"]), ("z", "x", "c", "y")
    )
    rows = ("z", "x", "c", "y")
    return jax.shard_map(
        shards,
        mesh=fine,
        in_specs=(P(rows, None), P(rows), P(None, rows), P(None, rows)),
        out_specs=(P(rows), P(rows), P()),
        check_vma=False,
    )
```
